128 devices in a mesh: bx: 16 (over z_hi, x, core), by: 8 (over z_lo, y).
Axes of the slice: x: 4, y: 4, z: 4 (z_hi: 2, z_lo: 2; z = z_hi * 2 + z_lo), core: 2. Of those that a mesh axis runs over, the one named last changes fastest.
Arguments:
- spectra: bfloat16 [16384, 10, 2, 256], P(('bx', 'by')), may hold values from -220 to 220, as said below
- band_edges: int32 [9], replicated, may hold values from 0 to 256, as said below
Outputs:
- stacked: float32 [16384, 6, 2, 8, 128], P(('bx', 'by'))
The draws below stay inside these ranges and needn't reach their ends.
Inputs may be any that keep to these rules, and one draw needn't show every extreme that they name: `spectra`: values of moderate size for every channel, window and bin. `band_edges`: Rising; the first entry is 0, the last is 256, and each band holds at least 16 bins.
All inputs are finite; a program needn't handle non-finite values.
Results may differ from the reference program's by a relative error of at most 0.0003.
Values may be sent and summed in bfloat16 or wider, within the bound.
A program may use at most 128 MiB of HBM per device.

```python
import math
import jax
import jax.numpy as jnp
from jax import lax

F = 256
W = 10
BANDS = 8
ROUNDS = 6
CH_DEV = 128
CHANNELS = 16384
N_BX = 16
N_BY = 8


def draw_spectra(key, part):
    key = jax.random.fold_in(key, 11)
    keys = jax.random.split(key, 3)
    shape = (CHANNELS, W, 2, F)
    rising = 3.0 ** (jnp.arange(CHANNELS, dtype=jnp.float32) / max(CHANNELS - 1, 1))
    base = jnp.clip(jax.random.normal(keys[0], shape, jnp.float32), -6.0, 6.0)
    rough = jnp.exp(jax.random.uniform(keys[1], (CHANNELS,), jnp.float32, 0.0, math.log(3.5)))
    bins = jnp.exp(jax.random.uniform(keys[2], (F,), jnp.float32, 0.0, math.log(3.0)))
    scale = (rising * rough)[:, None, None, None] * bins[None, None, None, :]
    return (base * scale).astype(jnp.bfloat16)


def draw_band_edges(key, part):
    key = jax.random.fold_in(key, 5)
    extra = jax.random.randint(key, (BANDS - 1,), 0, F // 16 + 1)
    cuts = jnp.cumsum(F // 16 + extra)
    return jnp.concatenate([jnp.zeros((1,), jnp.int32), cuts.astype(jnp.int32), jnp.full((1,), F, jnp.int32)])


def setup_inputs(seed: int = 0) -> dict:
    seeds = jax.random.split(jax.random.key(seed), 3)
    spectra = draw_spectra(jax.random.fold_in(seeds[2], 71), 0)
    band_edges = draw_band_edges(jax.random.fold_in(seeds[2], 71), 0)
    return dict(spectra=spectra, band_edges=band_edges)


EPS = 1e-6
HIGH = lax.Precision.HIGHEST


def reference(spectra, band_edges):
    values = spectra.astype(jnp.float32)
    freq = jnp.arange(F, dtype=jnp.int32)[None, :]
    inband = ((freq >= band_edges[:-1, None]) & (freq < band_edges[1:, None])).astype(jnp.float32)
    power_bins = jnp.sum(values * values, axis=(0, 1, 2))
    power = jnp.dot(inband, power_bins, precision=HIGH)
    norm = 1.0 / (power / (CHANNELS * W) + EPS)
    count = N_BX * N_BY
    logn = count.bit_length() - 1
    blocks = values.reshape(count, CH_DEV, W, 2, F)

    def one_block(index):
        own = lax.dynamic_index_in_dim(blocks, index, 0, keepdims=False)
        rounds_out = []
        for step in range(ROUNDS):
            bit = (logn - 1 - step) % logn
            other = jnp.bitwise_xor(index, jnp.int32(1 << bit)).astype(jnp.int32)
            peer = lax.dynamic_index_in_dim(blocks, other, 0, keepdims=False)
            real_bins = jnp.einsum("awf,bwf->fab", own[:, :, 0], peer[:, :, 0], precision=HIGH) + jnp.einsum("awf,bwf->fab", own[:, :, 1], peer[:, :, 1], precision=HIGH)
            imag_bins = jnp.einsum("awf,bwf->fab", own[:, :, 1], peer[:, :, 0], precision=HIGH) - jnp.einsum("awf,bwf->fab", own[:, :, 0], peer[:, :, 1], precision=HIGH)
            real = jnp.einsum("kf,fab->akb", inband, real_bins, precision=HIGH)
            imag = jnp.einsum("kf,fab->akb", inband, imag_bins, precision=HIGH)
            both = jnp.stack([real, imag], axis=1) * norm[None, None, :, None]
            rounds_out.append(both)
        return jnp.stack(rounds_out, axis=1)

    result = lax.map(one_block, jnp.arange(count, dtype=jnp.int32))
    return result.reshape(CHANNELS, ROUNDS, 2, BANDS, CH_DEV)
```

```python
import functools
import jax
import jax.numpy as jnp
from jax import lax
from jax.experimental import pallas as pl
from jax.experimental.pallas import tpu as pltpu
from jax.sharding import PartitionSpec as P

ROUNDS = 6
EPS = 1e-06
MESH = pl.DeviceIdType.MESH
AHEAD = 2
COMPUTE = True
COMM = True


def flip(index, bit):
    return index + bit - 2 * bit * ((index // bit) % 2)


def band_mask(edges_ref, bands, nbins):
    row = lax.broadcasted_iota(jnp.int32, (bands, nbins), 0)
    freq = lax.broadcasted_iota(jnp.int32, (bands, nbins), 1)
    low = jnp.zeros((bands, nbins), jnp.int32)
    high = jnp.zeros((bands, nbins), jnp.int32)
    for b in range(bands):
        low = jnp.where(row == b, edges_ref[b], low)
        high = jnp.where(row == b, edges_ref[b + 1], high)
    return jnp.where((freq >= low) & (freq < high), 1.0, 0.0).astype(jnp.float32)


def kernel(count, edges_ref, x_ref, acc_ref, norm_ref,
           xv, own, got, hop_a, hop_b, left, spread, power, parts,
           load_sem, send_sem, recv_sem, psend_sem, precv_sem):
    channels, windows, nparts, nbins = xv.shape
    bands = norm_ref.shape[0]
    bx, by = lax.axis_index("bx"), lax.axis_index("by")
    core = (flip(bx, 1), by)
    x1 = (flip(bx, 2), by)
    x3 = (flip(flip(bx, 2), 4), by)
    z1 = (bx, flip(by, 4))
    z3 = (flip(bx, 8), flip(by, 4))
    y1 = (bx, flip(by, 1))
    y3 = (bx, flip(flip(by, 1), 2))

    load = pltpu.make_async_copy(x_ref, xv, load_sem)
    load.start()

    barrier = pltpu.get_barrier_semaphore()
    neighbours = (core, x1, x3, z1, z3, y1, y3)
    for device in neighbours:
        pl.semaphore_signal(barrier, inc=1, device_id=device, device_id_type=MESH)

    def remote(stream, c, src, dst, device):
        return pltpu.make_async_remote_copy(
            src_ref=src, dst_ref=dst, send_sem=send_sem.at[stream, c],
            recv_sem=recv_sem.at[stream, c], device_id=device, device_id_type=MESH)

    half = pl.ds(0, channels), pl.ds(channels, channels)
    def copy(stream, c):
        if stream == 0:
            return remote(0, c, got.at[4, c], got.at[0, c], z3)
        if stream == 1:
            return remote(1, c, got.at[2, c], got.at[1, c], x3)
        if stream == 2:
            return remote(2, c, own.at[c], got.at[2, c], x1)
        if stream == 3:
            return remote(3, c, own.at[c], got.at[3, c], core)
        if stream == 4:
            return remote(4, c, own.at[c], got.at[4, c], z1)
        if stream == 5:
            return remote(5, c, hop_a.at[c], got.at[5, c, half[0]], y3)
        if stream == 6:
            return remote(6, c, own.at[c, half[0]], hop_a.at[c], y1)
        if stream == 7:
            return remote(7, c, own.at[c, half[1]], hop_b.at[c], y3)
        return remote(8, c, hop_b.at[c], got.at[5, c, half[1]], y1)

    rows = nparts * channels
    def prepare(c):
        block = xv[:, c].reshape(rows, nbins)
        r = lax.broadcasted_iota(jnp.int32, (rows, rows), 0)
        k = lax.broadcasted_iota(jnp.int32, (rows, rows), 1)
        pick = jnp.where(k == nparts * (r % channels) + r // channels, 1.0, 0.0).astype(jnp.bfloat16)
        own[c] = jnp.dot(pick, block, preferred_element_type=jnp.float32).astype(jnp.bfloat16)

    def send(c):
        for stream in (2, 4, 6, 7, 3):
            copy(stream, c).start()

    load.wait()
    prepare(0)
    pl.semaphore_wait(barrier, len(neighbours))
    if COMM: send(0)
    for c in range(1, AHEAD):
        prepare(c)
        if COMM: send(c)
    @pl.loop(AHEAD, windows)
    def _(c):
        prepare(c)

    mask = band_mask(edges_ref, bands, nbins)
    er = lax.broadcasted_iota(jnp.int32, spread.shape, 0)
    ek = lax.broadcasted_iota(jnp.int32, spread.shape, 1)
    spread[...] = jnp.where(ek == er // bands, 1.0, 0.0).astype(jnp.bfloat16)

    def squares(c, total):
        v = own[c].astype(jnp.float32)
        return total + jnp.sum((v * v).reshape(rows // 8, 8, nbins), axis=0)
    bins = lax.fori_loop(0, windows, squares, jnp.zeros((8, nbins), jnp.float32))
    bins = jnp.sum(bins, axis=0, keepdims=True)
    power[...] = jnp.broadcast_to(jnp.sum(mask * bins, axis=1, keepdims=True), power.shape)

    route = (core, x1, x3, z1, z3, y1, y3)
    def exchange(step):
        return pltpu.make_async_remote_copy(
            src_ref=parts.at[step], dst_ref=parts.at[len(route) + step], send_sem=psend_sem.at[step],
            recv_sem=precv_sem.at[step], device_id=route[step], device_id_type=MESH)

    def begin(step):
        parts[step] = power[...]
        exchange(step).start()

    def end(step):
        exchange(step).wait_recv()
        power[...] += parts[len(route) + step]

    begin(0)

    acc_ref[...] = jnp.zeros_like(acc_ref)

    def build(c):
        for p in range(nparts):
            wide = jnp.dot(spread[...], own[c, half[p]], preferred_element_type=jnp.float32)
            wide = wide.reshape(channels, bands, nbins) * mask[None]
            left[c, :, p * nbins:(p + 1) * nbins] = wide.reshape(channels * bands, nbins).astype(jnp.bfloat16)

    def accumulate(r, c):
        if not COMPUTE: return
        cos, sin = got[r, c, half[0]], got[r, c, half[1]]
        right = jnp.concatenate(
            [jnp.concatenate([cos, sin], axis=1), jnp.concatenate([-sin, cos], axis=1)], axis=0)
        acc_ref[r] += lax.dot_general(
            left[c], right, (((1,), (1,)), ((), ())), preferred_element_type=jnp.float32)

    def wait(stream, c):
        if COMM: copy(stream, c).wait_recv()

    def start(stream, c):
        if COMM: copy(stream, c).start()

    @pl.loop(0, windows)
    def _(c):
        if COMM:
            @pl.when(c + AHEAD < windows)
            def _():
                send(c + AHEAD)
        if COMPUTE: build(c)
        wait(2, c)
        start(1, c)
        wait(4, c)
        start(0, c)
        wait(6, c)
        start(5, c)
        wait(7, c)
        start(8, c)
        for step in range(len(route)):
            @pl.when(c == step + 1)
            def _(step=step):
                end(step)
                if step + 1 < len(route):
                    begin(step + 1)
        wait(3, c)
        accumulate(3, c)
        accumulate(2, c)
        accumulate(4, c)

        @pl.when(c > 0)
        def _():
            for r in (1, 0, 5):
                wait(r, c - 1)
                if r == 5:
                    wait(8, c - 1)
                accumulate(r, c - 1)

    for r in (1, 0, 5):
        wait(r, windows - 1)
        if r == 5:
            wait(8, windows - 1)
        accumulate(r, windows - 1)

    norm_ref[...] = 1.0 / (power[...] / (count * windows) + EPS)
    if COMM:
        @pl.loop(0, windows)
        def _(c):
            for stream in range(9):
                copy(stream, c).wait_send()
    for step in range(len(route)):
        exchange(step).wait_send()


def finish(acc_ref, norm_ref, out_ref):
    norm = norm_ref[...]
    for r in range(ROUNDS):
        for p in range(2):
            lanes = norm.shape[1]
            block = acc_ref[r, :, p * lanes:(p + 1) * lanes]
            out_ref[:, r, p] = block.reshape(-1, *norm.shape) * norm[None]


def body(spectra, band_edges):
    channels, windows, parts, nbins = spectra.shape
    bands = band_edges.shape[0] - 1
    devices = lax.axis_size("bx") * lax.axis_size("by")
    rows = channels * parts
    dma = pltpu.SemaphoreType.DMA
    vmem = pltpu.VMEM
    acc, norm = pl.pallas_call(
        functools.partial(kernel, channels * devices),
        out_shape=(vmem((ROUNDS, channels * bands, parts * channels), jnp.float32),
                   vmem((bands, 128), jnp.float32)),
        in_specs=[pl.BlockSpec(memory_space=pltpu.SMEM), pl.BlockSpec(memory_space=pl.ANY)],
        out_specs=(pl.BlockSpec(memory_space=vmem), pl.BlockSpec(memory_space=vmem)),
        scratch_shapes=[
            vmem(spectra.shape, jnp.bfloat16),
            vmem((windows, rows, nbins), jnp.bfloat16),
            vmem((ROUNDS, windows, rows, nbins), jnp.bfloat16),
            vmem((windows, channels, nbins), jnp.bfloat16),
            vmem((windows, channels, nbins), jnp.bfloat16),
            vmem((windows, channels * bands, parts * nbins), jnp.bfloat16),
            vmem((channels * bands, channels), jnp.bfloat16),
            vmem((bands, 128), jnp.float32),
            vmem((14, bands, 128), jnp.float32),
            dma(()), dma((9, windows)), dma((9, windows)), dma((7,)), dma((7,)),
        ],
        compiler_params=pltpu.CompilerParams(
            collective_id=0, has_side_effects=True, vmem_limit_bytes=48 * 2**20),
        name="exchange",
    )(band_edges, spectra)
    tile = 16
    return pl.pallas_call(
        finish,
        grid=(channels // tile,),
        out_shape=jax.ShapeDtypeStruct((channels, ROUNDS, parts, bands, channels), jnp.float32),
        in_specs=[pl.BlockSpec((ROUNDS, tile * bands, parts * channels), lambda i: (0, i, 0)),
                  pl.BlockSpec((bands, 128), lambda i: (0, 0))],
        out_specs=pl.BlockSpec((tile, ROUNDS, parts, bands, channels), lambda i: (i, 0, 0, 0, 0)),
        name="finish",
    )(acc, norm)


def solution(mesh):
    return jax.shard_map(
        body,
        mesh=mesh,
        in_specs=(P(("bx", "by"), None, None, None), P()),
        out_specs=P(("bx", "by"), None, None, None, None),
        check_vma=False,
    )
```

```python
import functools
import jax
import jax.numpy as jnp
from jax import lax
from jax.experimental import pallas as pl
from jax.experimental.pallas import tpu as pltpu
from jax.sharding import PartitionSpec as P

ROUNDS = 6
EPS = 1e-06
MESH = pl.DeviceIdType.MESH
AHEAD = 2
COMPUTE = True
COMM = True


def flip(index, bit):
    return index + bit - 2 * bit * ((index // bit) % 2)


def band_mask(edges_ref, bands, nbins):
    row = lax.broadcasted_iota(jnp.int32, (bands, nbins), 0)
    freq = lax.broadcasted_iota(jnp.int32, (bands, nbins), 1)
    low = jnp.zeros((bands, nbins), jnp.int32)
    high = jnp.zeros((bands, nbins), jnp.int32)
    for b in range(bands):
        low = jnp.where(row == b, edges_ref[b], low)
        high = jnp.where(row == b, edges_ref[b + 1], high)
    return jnp.where((freq >= low) & (freq < high), 1.0, 0.0).astype(jnp.float32)


def kernel(count, edges_ref, x_ref, acc_ref, norm_ref,
           xv, own, got, hop_a, hop_b, left, spread, power, parts,
           load_sem, send_sem, recv_sem, psend_sem, precv_sem):
    channels, windows, nparts, nbins = xv.shape
    bands = norm_ref.shape[0]
    bx, by = lax.axis_index("bx"), lax.axis_index("by")
    core = (flip(bx, 1), by)
    x1 = (flip(bx, 2), by)
    x3 = (flip(flip(bx, 2), 4), by)
    z1 = (bx, flip(by, 4))
    z3 = (flip(bx, 8), flip(by, 4))
    y1 = (bx, flip(by, 1))
    y3 = (bx, flip(flip(by, 1), 2))

    load = pltpu.make_async_copy(x_ref, xv, load_sem)
    load.start()

    barrier = pltpu.get_barrier_semaphore()
    neighbours = (core, x1, x3, z1, z3, y1, y3)
    for device in neighbours:
        pl.semaphore_signal(barrier, inc=1, device_id=device, device_id_type=MESH)

    def remote(stream, c, src, dst, device):
        return pltpu.make_async_remote_copy(
            src_ref=src, dst_ref=dst, send_sem=send_sem.at[stream, c],
            recv_sem=recv_sem.at[stream, c], device_id=device, device_id_type=MESH)

    half = pl.ds(0, channels), pl.ds(channels, channels)
    def copy(stream, c):
        if stream == 0:
            return remote(0, c, got.at[4, c], got.at[0, c], z3)
        if stream == 1:
            return remote(1, c, got.at[2, c], got.at[1, c], x3)
        if stream == 2:
            return remote(2, c, own.at[c], got.at[2, c], x1)
        if stream == 3:
            return remote(3, c, own.at[c], got.at[3, c], core)
        if stream == 4:
            return remote(4, c, own.at[c], got.at[4, c], z1)
        if stream == 5:
            return remote(5, c, hop_a.at[c], got.at[5, c, half[0]], y3)
        if stream == 6:
            return remote(6, c, own.at[c, half[0]], hop_a.at[c], y1)
        if stream == 7:
            return remote(7, c, own.at[c, half[1]], hop_b.at[c], y3)
        return remote(8, c, hop_b.at[c], got.at[5, c, half[1]], y1)

    rows = nparts * channels
    def prepare(c):
        block = xv[:, c].reshape(rows, nbins)
        r = lax.broadcasted_iota(jnp.int32, (rows, rows), 0)
        k = lax.broadcasted_iota(jnp.int32, (rows, rows), 1)
        pick = jnp.where(k == nparts * (r % channels) + r // channels, 1.0, 0.0).astype(jnp.bfloat16)
        own[c] = jnp.dot(pick, block, preferred_element_type=jnp.float32).astype(jnp.bfloat16)

    def send(c):
        for stream in (2, 4, 6, 7, 3):
            copy(stream, c).start()

    load.wait()
    prepare(0)
    pl.semaphore_wait(barrier, len(neighbours))
    if COMM: send(0)
    for c in range(1, AHEAD):
        prepare(c)
        if COMM: send(c)
    @pl.loop(AHEAD, windows)
    def _(c):
        prepare(c)

    mask = band_mask(edges_ref, bands, nbins)
    er = lax.broadcasted_iota(jnp.int32, spread.shape, 0)
    ek = lax.broadcasted_iota(jnp.int32, spread.shape, 1)
    spread[...] = jnp.where(ek == er // bands, 1.0, 0.0).astype(jnp.bfloat16)

    def squares(c, total):
        v = own[c].astype(jnp.float32)
        return total + jnp.sum((v * v).reshape(rows // 8, 8, nbins), axis=0)
    bins = lax.fori_loop(0, windows, squares, jnp.zeros((8, nbins), jnp.float32))
    bins = jnp.sum(bins, axis=0, keepdims=True)
    power[...] = jnp.broadcast_to(jnp.sum(mask * bins, axis=1, keepdims=True), power.shape)

    route = (core, x1, x3, z1, z3, y1, y3)
    def exchange(step):
        return pltpu.make_async_remote_copy(
            src_ref=parts.at[step], dst_ref=parts.at[len(route) + step], send_sem=psend_sem.at[step],
            recv_sem=precv_sem.at[step], device_id=route[step], device_id_type=MESH)

    def begin(step):
        parts[step] = power[...]
        exchange(step).start()

    def end(step):
        exchange(step).wait_recv()
        power[...] += parts[len(route) + step]

    begin(0)

    acc_ref[...] = jnp.zeros_like(acc_ref)

    def build(c):
        for p in range(nparts):
            wide = jnp.dot(spread[...], own[c, half[p]], preferred_element_type=jnp.float32)
            wide = wide.reshape(channels, bands, nbins) * mask[None]
            left[c, :, p * nbins:(p + 1) * nbins] = wide.reshape(channels * bands, nbins).astype(jnp.bfloat16)

    def accumulate(r, c):
        if not COMPUTE: return
        cos, sin = got[r, c, half[0]], got[r, c, half[1]]
        right = jnp.concatenate(
            [jnp.concatenate([cos, sin], axis=1), jnp.concatenate([-sin, cos], axis=1)], axis=0)
        acc_ref[r] += lax.dot_general(
            left[c], right, (((1,), (1,)), ((), ())), preferred_element_type=jnp.float32)

    def wait(stream, c):
        if COMM: copy(stream, c).wait_recv()

    def start(stream, c):
        if COMM: copy(stream, c).start()

    @pl.loop(0, windows)
    def _(c):
        if COMM:
            @pl.when(c + AHEAD < windows)
            def _():
                send(c + AHEAD)
        if COMPUTE: build(c)
        wait(2, c)
        start(1, c)
        wait(4, c)
        start(0, c)
        wait(6, c)
        start(5, c)
        wait(7, c)
        start(8, c)
        for step in range(len(route)):
            @pl.when(c == step + 1)
            def _(step=step):
                end(step)
                if step + 1 < len(route):
                    begin(step + 1)
        wait(3, c)
        accumulate(3, c)
        accumulate(2, c)
        accumulate(4, c)

        @pl.when(c > 0)
        def _():
            for r in (1, 0, 5):
                wait(r, c - 1)
                if r == 5:
                    wait(8, c - 1)
                accumulate(r, c - 1)

    for r in (1, 0, 5):
        wait(r, windows - 1)
        if r == 5:
            wait(8, windows - 1)
        accumulate(r, windows - 1)

    norm_ref[...] = 1.0 / (power[...] / (count * windows) + EPS)
    if COMM:
        @pl.loop(0, windows)
        def _(c):
            for stream in range(9):
                copy(stream, c).wait_send()
    for step in range(len(route)):
        exchange(step).wait_send()


def finish(acc_ref, norm_ref, out_ref):
    norm = norm_ref[...]
    size = out_ref.shape[0] * norm.shape[0]
    rows = pl.ds(pl.multiple_of(pl.program_id(0) * size, size), size)
    for r in range(ROUNDS):
        for p in range(2):
            lanes = norm.shape[1]
            block = acc_ref[r, rows, p * lanes:(p + 1) * lanes]
            out_ref[:, r, p] = block.reshape(-1, *norm.shape) * norm[None]


def body(spectra, band_edges):
    channels, windows, parts, nbins = spectra.shape
    bands = band_edges.shape[0] - 1
    devices = lax.axis_size("bx") * lax.axis_size("by")
    rows = channels * parts
    dma = pltpu.SemaphoreType.DMA
    vmem = pltpu.VMEM
    acc, norm = pl.pallas_call(
        functools.partial(kernel, channels * devices),
        out_shape=(vmem((ROUNDS, channels * bands, parts * channels), jnp.float32),
                   vmem((bands, 128), jnp.float32)),
        in_specs=[pl.BlockSpec(memory_space=pltpu.SMEM), pl.BlockSpec(memory_space=pl.ANY)],
        out_specs=(pl.BlockSpec(memory_space=vmem), pl.BlockSpec(memory_space=vmem)),
        scratch_shapes=[
            vmem(spectra.shape, jnp.bfloat16),
            vmem((windows, rows, nbins), jnp.bfloat16),
            vmem((ROUNDS, windows, rows, nbins), jnp.bfloat16),
            vmem((windows, channels, nbins), jnp.bfloat16),
            vmem((windows, channels, nbins), jnp.bfloat16),
            vmem((windows, channels * bands, parts * nbins), jnp.bfloat16),
            vmem((channels * bands, channels), jnp.bfloat16),
            vmem((bands, 128), jnp.float32),
            vmem((14, bands, 128), jnp.float32),
            dma(()), dma((9, windows)), dma((9, windows)), dma((7,)), dma((7,)),
        ],
        compiler_params=pltpu.CompilerParams(
            collective_id=0, has_side_effects=True, vmem_limit_bytes=48 * 2**20),
        name="exchange",
    )(band_edges, spectra)
    tile = 16
    return pl.pallas_call(
        finish,
        grid=(channels // tile,),
        out_shape=jax.ShapeDtypeStruct((channels, ROUNDS, parts, bands, channels), jnp.float32),
        in_specs=[pl.BlockSpec(memory_space=vmem), pl.BlockSpec(memory_space=vmem)],
        out_specs=pl.BlockSpec((tile, ROUNDS, parts, bands, channels), lambda i: (i, 0, 0, 0, 0)),
        compiler_params=pltpu.CompilerParams(vmem_limit_bytes=16 * 2**20),
        name="finish",
    )(*(pltpu.with_memory_space_constraint(v, vmem) for v in (acc, norm)))


def solution(mesh):
    return jax.shard_map(
        body,
        mesh=mesh,
        in_specs=(P(("bx", "by"), None, None, None), P()),
        out_specs=P(("bx", "by"), None, None, None, None),
        check_vma=False,
    )
```

```python
import functools
import jax
import jax.numpy as jnp
from jax import lax
from jax.experimental import pallas as pl
from jax.experimental.pallas import tpu as pltpu
from jax.sharding import PartitionSpec as P

ROUNDS = 6
EPS = 1e-06
MESH = pl.DeviceIdType.MESH
AHEAD = 2
COMPUTE = True
COMM = True


def flip(index, bit):
    return index + bit - 2 * bit * ((index // bit) % 2)


def band_mask(edges_ref, bands, nbins):
    row = lax.broadcasted_iota(jnp.int32, (bands, nbins), 0)
    freq = lax.broadcasted_iota(jnp.int32, (bands, nbins), 1)
    low = jnp.zeros((bands, nbins), jnp.int32)
    high = jnp.zeros((bands, nbins), jnp.int32)
    for b in range(bands):
        low = jnp.where(row == b, edges_ref[b], low)
        high = jnp.where(row == b, edges_ref[b + 1], high)
    return jnp.where((freq >= low) & (freq < high), 1.0, 0.0).astype(jnp.float32)


def kernel(count, edges_ref, x_ref, acc_ref, xv, own, got, left, power, parts,
           load_sem, send_sem, recv_sem, psend_sem, precv_sem):
    channels, windows, nparts, nbins = xv.shape
    bands = power.shape[0]
    rows = nparts * channels
    bx, by = lax.axis_index("bx"), lax.axis_index("by")
    core = (flip(bx, 1), by)
    x1 = (flip(bx, 2), by)
    x3 = (flip(flip(bx, 2), 4), by)
    z1 = (bx, flip(by, 4))
    z3 = (flip(bx, 8), flip(by, 4))
    y1 = (bx, flip(by, 1))
    y2 = (bx, flip(by, 2))

    def load(c):
        return pltpu.make_async_copy(x_ref.at[:, pl.ds(c, 1)], xv.at[:, pl.ds(c, 1)], load_sem.at[c])

    for c in range(windows):
        load(c).start()

    barrier = pltpu.get_barrier_semaphore()
    ring_x = (core, x1, x3, (flip(bx, 4), by))
    ring_x = ring_x + tuple((flip(device[0], 1), by) for device in ring_x[1:])
    ring_z = (z1, z3, (flip(bx, 8), by))
    ring_y = (y1, y2, (bx, flip(flip(by, 1), 2)))
    neighbours = ring_x + ring_z + ring_y
    for device in neighbours:
        pl.semaphore_signal(barrier, inc=1, device_id=device, device_id_type=MESH)

    def copy(stream, c):
        src = {0: got.at[4, c], 1: got.at[2, c]}.get(stream, own.at[c])
        return pltpu.make_async_remote_copy(
            src_ref=src, dst_ref=got.at[stream, c], send_sem=send_sem.at[stream, c],
            recv_sem=recv_sem.at[stream, c], device_id=(z3, x3, x1, core, z1, y2)[stream], device_id_type=MESH)

    r = lax.broadcasted_iota(jnp.int32, (rows, rows), 0)
    k = lax.broadcasted_iota(jnp.int32, (rows, rows), 1)
    pick = jnp.where(k == nparts * (r % channels) + r // channels, 1.0, 0.0).astype(jnp.bfloat16)

    def prepare(c):
        load(c).wait()
        block = xv[:, c].reshape(rows, nbins)
        own[c] = jnp.dot(pick, block, preferred_element_type=jnp.float32).astype(jnp.bfloat16)

    def send(c):
        if COMM:
            for stream in (2, 4, 5, 3):
                copy(stream, c).start()

    for c in range(windows):
        prepare(c)
        if c == 0:
            pl.semaphore_wait(barrier, len(neighbours))
        if c < AHEAD:
            send(c)

    mask = band_mask(edges_ref, bands, nbins)

    def measure():
        def squares(c, total):
            v = own[c].astype(jnp.float32)
            return total + jnp.sum((v * v).reshape(rows // 8, 8, nbins), axis=0)
        bins = lax.fori_loop(0, windows, squares, jnp.zeros((8, nbins), jnp.float32))
        bins = jnp.sum(bins, axis=0, keepdims=True)
        power[...] = jnp.broadcast_to(jnp.sum(mask * bins, axis=1, keepdims=True), power.shape)

    def exchange(i):
        return pltpu.make_async_remote_copy(
            src_ref=parts.at[i], dst_ref=parts.at[len(neighbours) + i], send_sem=psend_sem.at[i],
            recv_sem=precv_sem.at[i], device_id=neighbours[i], device_id_type=MESH)

    stages = (range(7), range(7, 10), range(10, 13))

    def begin(stage):
        for i in stage:
            parts[i] = power[...]
            exchange(i).start()

    def end(stage):
        for i in stage:
            exchange(i).wait_recv()
            power[...] += parts[len(neighbours) + i]


    def build(c):
        for p in range(nparts):
            v = own[c, p * channels:(p + 1) * channels].astype(jnp.float32)
            wide = jnp.broadcast_to(v[:, None, :], (channels, bands, nbins)) * mask[None]
            left[c, :, p * nbins:(p + 1) * nbins] = wide.reshape(channels * bands, nbins).astype(jnp.bfloat16)

    def accumulate(r, c, norm=None):
        if not COMPUTE: return
        cos, sin = got[r, c, :channels], got[r, c, channels:]
        right = jnp.concatenate(
            [jnp.concatenate([cos, sin], axis=1), jnp.concatenate([-sin, cos], axis=1)], axis=0)
        product = lax.dot_general(
            left[c], right, (((1,), (1,)), ((), ())), preferred_element_type=jnp.float32)
        for p in range(2):
            value = acc_ref[:, r, p] + product[:, p * channels:(p + 1) * channels].reshape(
                channels, bands, channels)
            if norm is not None:
                value = value * norm[None]
            acc_ref[:, r, p] = value

    def wait(stream, c):
        if COMM: copy(stream, c).wait_recv()

    def start(stream, c):
        if COMM: copy(stream, c).start()

    def advance(c):
        if COMM:
            @pl.when(c + AHEAD < windows)
            def _():
                send(c + AHEAD)
        wait(2, c)
        start(1, c)
        wait(4, c)
        start(0, c)

    direct, passed = (3, 2, 4, 5), (1, 0)
    measure()
    begin(stages[0])
    if COMPUTE: build(0)
    acc_ref[...] = jnp.zeros_like(acc_ref)
    advance(0)
    if COMPUTE: build(1)
    advance(1)
    wait(3, 0)
    wait(5, 0)
    for r in direct:
        accumulate(r, 0)

    @pl.loop(2, windows)
    def _(c):
        advance(c)
        for step in range(len(stages)):
            @pl.when(c == 2 * step + 3)
            def _(step=step):
                end(stages[step])
                if step + 1 < len(stages):
                    begin(stages[step + 1])
        wait(3, c - 1)
        wait(5, c - 1)
        for r in passed:
            wait(r, c - 2)
        if COMPUTE: build(c)
        for r in direct:
            accumulate(r, c - 1)
        for r in passed:
            accumulate(r, c - 2)

    norm = 1.0 / (power[...] / (count * windows) + EPS)
    last = windows - 1
    for r in passed:
        wait(r, last - 1)
        accumulate(r, last - 1)
    wait(3, last)
    wait(5, last)
    for r in direct:
        accumulate(r, last, norm)
    for r in passed:
        wait(r, last)
    for r in passed:
        accumulate(r, last, norm)

    if COMM:
        @pl.loop(0, windows)
        def _(c):
            for stream in range(ROUNDS):
                copy(stream, c).wait_send()
    for i in range(len(neighbours)):
        exchange(i).wait_send()


def body(spectra, band_edges):
    channels, windows, parts, nbins = spectra.shape
    bands = band_edges.shape[0] - 1
    devices = lax.axis_size("bx") * lax.axis_size("by")
    rows = channels * parts
    dma = pltpu.SemaphoreType.DMA
    vmem = pltpu.VMEM
    return pl.pallas_call(
        functools.partial(kernel, channels * devices),
        out_shape=vmem((channels, ROUNDS, parts, bands, channels), jnp.float32),
        in_specs=[pl.BlockSpec(memory_space=pltpu.SMEM), pl.BlockSpec(memory_space=pl.ANY)],
        out_specs=pl.BlockSpec(memory_space=vmem),
        scratch_shapes=[
            vmem(spectra.shape, jnp.bfloat16),
            vmem((windows, rows, nbins), jnp.bfloat16),
            vmem((ROUNDS, windows, rows, nbins), jnp.bfloat16),
            vmem((windows, channels * bands, parts * nbins), jnp.bfloat16),
            vmem((bands, 128), jnp.float32),
            vmem((26, bands, 128), jnp.float32),
            dma((windows,)), dma((ROUNDS, windows)), dma((ROUNDS, windows)), dma((13,)), dma((13,)),
        ],
        compiler_params=pltpu.CompilerParams(
            collective_id=0, has_side_effects=True, vmem_limit_bytes=48 * 2**20),
        name="exchange",
    )(band_edges, spectra)


def solution(mesh):
    return jax.shard_map(
        body,
        mesh=mesh,
        in_specs=(P(("bx", "by"), None, None, None), P()),
        out_specs=P(("bx", "by"), None, None, None, None),
        check_vma=False,
    )
```

```python
import functools
import jax
import jax.numpy as jnp
from jax import lax
from jax.experimental import pallas as pl
from jax.experimental.pallas import tpu as pltpu
from jax.sharding import PartitionSpec as P

ROUNDS = 6
EPS = 1e-06
MESH = pl.DeviceIdType.MESH
AHEAD = 2
COMPUTE = True
COMM = True


def flip(index, bit):
    return index + bit - 2 * bit * ((index // bit) % 2)


def band_mask(edges_ref, bands, nbins):
    row = lax.broadcasted_iota(jnp.int32, (bands, nbins), 0)
    freq = lax.broadcasted_iota(jnp.int32, (bands, nbins), 1)
    low = jnp.zeros((bands, nbins), jnp.int32)
    high = jnp.zeros((bands, nbins), jnp.int32)
    for b in range(bands):
        low = jnp.where(row == b, edges_ref[b], low)
        high = jnp.where(row == b, edges_ref[b + 1], high)
    return jnp.where((freq >= low) & (freq < high), 1.0, 0.0).astype(jnp.float32)


def kernel(count, edges_ref, x_ref, acc_ref, wide_ref, right_ref, norm_ref, xv, own, got, left, power, parts,
           load_sem, send_sem, recv_sem, psend_sem, precv_sem):
    channels, windows, nparts, nbins = xv.shape
    bands = power.shape[0]
    rows = nparts * channels
    bx, by = lax.axis_index("bx"), lax.axis_index("by")
    core = (flip(bx, 1), by)
    x1 = (flip(bx, 2), by)
    x3 = (flip(flip(bx, 2), 4), by)
    z1 = (bx, flip(by, 4))
    z3 = (flip(bx, 8), flip(by, 4))
    y1 = (bx, flip(by, 1))
    y2 = (bx, flip(by, 2))

    def load(c):
        return pltpu.make_async_copy(x_ref.at[:, pl.ds(c, 1)], xv.at[:, pl.ds(c, 1)], load_sem.at[c])

    load(0).start()
    barrier = pltpu.get_barrier_semaphore()
    ring_x = (core, x1, x3, (flip(bx, 4), by))
    ring_x = ring_x + tuple((flip(device[0], 1), by) for device in ring_x[1:])
    ring_z = (z1, z3, (flip(bx, 8), by))
    ring_y = (y1, y2, (bx, flip(flip(by, 1), 2)))
    neighbours = ring_x + ring_z + ring_y
    for device in neighbours:
        pl.semaphore_signal(barrier, inc=1, device_id=device, device_id_type=MESH)

    for c in range(1, windows):
        load(c).start()


    def copy(stream, c):
        src = {0: got.at[4, c], 1: got.at[2, c]}.get(stream, own.at[c])
        return pltpu.make_async_remote_copy(
            src_ref=src, dst_ref=got.at[stream, c], send_sem=send_sem.at[stream, c],
            recv_sem=recv_sem.at[stream, c], device_id=(z3, x3, x1, core, z1, y2)[stream], device_id_type=MESH)

    r = lax.broadcasted_iota(jnp.int32, (rows, rows), 0)
    k = lax.broadcasted_iota(jnp.int32, (rows, rows), 1)
    pick = jnp.where(k == nparts * (r % channels) + r // channels, 1.0, 0.0).astype(jnp.bfloat16)

    def prepare(c):
        load(c).wait()
        block = xv[:, c].reshape(rows, nbins)
        own[c] = jnp.dot(pick, block, preferred_element_type=jnp.float32).astype(jnp.bfloat16)

    def send(c):
        if COMM:
            for stream in (2, 4, 5):
                copy(stream, c).start()

    for c in range(windows):
        prepare(c)
        if c == 0:
            pl.semaphore_wait(barrier, len(neighbours))
        if c < AHEAD:
            send(c)
        if COMM:
            copy(3, c).start()

    mask = band_mask(edges_ref, bands, nbins)

    def measure():
        def squares(c, total):
            v = own[c].astype(jnp.float32)
            return total + jnp.sum((v * v).reshape(rows // 8, 8, nbins), axis=0)
        bins = lax.fori_loop(0, windows, squares, jnp.zeros((8, nbins), jnp.float32))
        bins = jnp.sum(bins, axis=0, keepdims=True)
        power[...] = jnp.broadcast_to(jnp.sum(mask * bins, axis=1, keepdims=True), power.shape)

    def exchange(i):
        return pltpu.make_async_remote_copy(
            src_ref=parts.at[i], dst_ref=parts.at[len(neighbours) + i], send_sem=psend_sem.at[i],
            recv_sem=precv_sem.at[i], device_id=neighbours[i], device_id_type=MESH)

    stages = (range(7), range(7, 10), range(10, 13))

    def begin(stage):
        for i in stage:
            parts[i] = power[...]
            exchange(i).start()

    def end(stage):
        for i in stage:
            exchange(i).wait_recv()
            power[...] += parts[len(neighbours) + i]


    def build(c):
        for p in range(nparts):
            v = own[c, p * channels:(p + 1) * channels].astype(jnp.float32)
            wide = jnp.broadcast_to(v[:, None, :], (channels, bands, nbins)) * mask[None]
            left[c, :, p * nbins:(p + 1) * nbins] = wide.reshape(channels * bands, nbins).astype(jnp.bfloat16)

    def paired(r, c):
        cos, sin = got[r, c, :channels], got[r, c, channels:]
        return jnp.concatenate(
            [jnp.concatenate([cos, sin], axis=1), jnp.concatenate([-sin, cos], axis=1)], axis=0)

    def accumulate(r, c, norm=None, width=1):
        if not COMPUTE: return
        right = jnp.concatenate([paired(r, c + i) for i in range(width)], axis=1)
        wide = jnp.concatenate([left[c + i] for i in range(width)], axis=1)
        product = lax.dot_general(
            wide, right, (((1,), (1,)), ((), ())), preferred_element_type=jnp.float32)
        for p in range(2):
            value = acc_ref[:, r, p] + product[:, p * channels:(p + 1) * channels].reshape(
                channels, bands, channels)
            if norm is not None:
                value = value * norm[None]
            acc_ref[:, r, p] = value

    def wait(stream, c):
        if COMM: copy(stream, c).wait_recv()

    def start(stream, c):
        if COMM: copy(stream, c).start()

    def advance(c):
        if COMM:
            @pl.when(c + AHEAD < windows)
            def _():
                send(c + AHEAD)
        wait(2, c)
        start(1, c)
        wait(4, c)
        start(0, c)

    def builds(first, count):
        if COMPUTE:
            @pl.loop(first, first + count)
            def _(c):
                build(c)

    def step(c, pair):
        advance(c)
        for i in range(len(stages) - 1):
            @pl.when(c == 3 * i + 4)
            def _(i=i):
                end(stages[i])
                begin(stages[i + 1])
        if pair:
            wait(3, 2 * c - 2)
            wait(3, 2 * c - 1)
        wait(5, c - 1)
        for r in (1, 0):
            wait(r, c - 2)
        for r in (2, 4, 5):
            accumulate(r, c - 1)
        for r in (1, 0):
            accumulate(r, c - 2)
        if pair:
            accumulate(3, 2 * c - 2, width=2)

    measure()
    begin(stages[0])
    advance(0)
    acc_ref[...] = jnp.zeros_like(acc_ref)
    builds(0, windows // 2)
    advance(1)
    builds(windows // 2, windows - windows // 2)
    wait(3, 0)
    wait(3, 1)
    for r in (2, 4):
        accumulate(r, 0)
    wait(5, 0)
    accumulate(5, 0)
    accumulate(3, 0, width=2)

    half = windows // 2 + 1
    @pl.loop(2, half)
    def _(c):
        step(c, True)

    @pl.loop(half, windows)
    def _(c):
        step(c, False)

    last = windows - 1
    end(stages[-1])
    norm = 1.0 / (power[...] / (count * windows) + EPS)
    wait(5, last)
    for r in (1, 0):
        wait(r, last - 1)
    for r in (2, 4, 5):
        accumulate(r, last, norm)
    for r in (1, 0):
        accumulate(r, last - 1)
    for p in range(2):
        acc_ref[:, 3, p] = acc_ref[:, 3, p] * norm[None]
    norm_ref[...] = norm
    wide_ref[...] = left[last]
    for r in (1, 0):
        wait(r, last)
        right_ref[r] = paired(r, last)

    if COMM:
        @pl.loop(0, windows)
        def _(c):
            for stream in range(ROUNDS):
                copy(stream, c).wait_send()
    for i in range(len(neighbours)):
        exchange(i).wait_send()


def finish(acc_ref, wide_ref, right_ref, norm_ref, out_ref, done, sems):
    channels, _, parts, bands, _ = acc_ref.shape
    count = done.shape[0]
    early = pltpu.make_async_copy(acc_ref.at[:, count:], out_ref.at[:, count:], sems.at[count])
    early.start()
    norm = norm_ref[...]
    late = []
    for r in range(count):
        product = lax.dot_general(
            wide_ref[...], right_ref[r], (((1,), (1,)), ((), ())), preferred_element_type=jnp.float32)
        for p in range(parts):
            value = product[:, p * channels:(p + 1) * channels].reshape(channels, bands, channels)
            done[r, :, p] = (acc_ref[:, r, p] + value) * norm[None]
        late.append(pltpu.make_async_copy(done.at[r], out_ref.at[:, r], sems.at[r]))
        late[-1].start()
    for copy in (early, *late):
        copy.wait()


def body(spectra, band_edges):
    channels, windows, parts, nbins = spectra.shape
    bands = band_edges.shape[0] - 1
    devices = lax.axis_size("bx") * lax.axis_size("by")
    rows = channels * parts
    dma = pltpu.SemaphoreType.DMA
    vmem = pltpu.VMEM
    results = pl.pallas_call(
        functools.partial(kernel, channels * devices),
        out_shape=(vmem((channels, ROUNDS, parts, bands, channels), jnp.float32),
                   vmem((channels * bands, parts * nbins), jnp.bfloat16),
                   vmem((2, rows, parts * nbins), jnp.bfloat16),
                   vmem((bands, 128), jnp.float32)),
        in_specs=[pl.BlockSpec(memory_space=pltpu.SMEM), pl.BlockSpec(memory_space=pl.ANY)],
        out_specs=(pl.BlockSpec(memory_space=vmem),) * 4,
        scratch_shapes=[
            vmem(spectra.shape, jnp.bfloat16),
            vmem((windows, rows, nbins), jnp.bfloat16),
            vmem((ROUNDS, windows, rows, nbins), jnp.bfloat16),
            vmem((windows, channels * bands, parts * nbins), jnp.bfloat16),
            vmem((bands, 128), jnp.float32),
            vmem((26, bands, 128), jnp.float32),
            dma((windows,)), dma((ROUNDS, windows)), dma((ROUNDS, windows)), dma((13,)), dma((13,)),
        ],
        compiler_params=pltpu.CompilerParams(
            collective_id=0, has_side_effects=True, vmem_limit_bytes=52 * 2**20),
        name="exchange",
    )(band_edges, spectra)
    return pl.pallas_call(
        finish,
        out_shape=jax.ShapeDtypeStruct((channels, ROUNDS, parts, bands, channels), jnp.float32),
        in_specs=[pl.BlockSpec(memory_space=vmem)] * 4,
        out_specs=pl.BlockSpec(memory_space=pl.ANY),
        scratch_shapes=[vmem((2, channels, parts, bands, channels), jnp.float32), dma((3,))],
        compiler_params=pltpu.CompilerParams(vmem_limit_bytes=8 * 2**20),
        name="finish",
    )(*(pltpu.with_memory_space_constraint(value, vmem) for value in results))


def solution(mesh):
    return jax.shard_map(
        body,
        mesh=mesh,
        in_specs=(P(("bx", "by"), None, None, None), P()),
        out_specs=P(("bx", "by"), None, None, None, None),
        check_vma=False,
    )
```

```python
import functools
import jax
import jax.numpy as jnp
from jax import lax
from jax.experimental import pallas as pl
from jax.experimental.pallas import tpu as pltpu
from jax.sharding import PartitionSpec as P

ROUNDS = 6
EPS = 1e-06
MESH = pl.DeviceIdType.MESH
AHEAD = 2
EARLY = 4
AT = (3, 6)
START = 3
COMPUTE = True
COMM = True


def flip(index, bit):
    return index + bit - 2 * bit * ((index // bit) % 2)


def band_mask(edges_ref, bands, nbins):
    row = lax.broadcasted_iota(jnp.int32, (bands, nbins), 0)
    freq = lax.broadcasted_iota(jnp.int32, (bands, nbins), 1)
    low = jnp.zeros((bands, nbins), jnp.int32)
    high = jnp.zeros((bands, nbins), jnp.int32)
    for b in range(bands):
        low = jnp.where(row == b, edges_ref[b], low)
        high = jnp.where(row == b, edges_ref[b + 1], high)
    return jnp.where((freq >= low) & (freq < high), 1.0, 0.0).astype(jnp.float32)


def kernel(count, edges_hbm, x_ref, acc_ref, wide_ref, right_ref, norm_ref, edges_ref, xv, own, got, left, power, parts,
           edges_sem, load_sem, send_sem, recv_sem, psend_sem, precv_sem):
    channels, windows, nparts, nbins = xv.shape
    bands = power.shape[0]
    rows = nparts * channels
    bx, by = lax.axis_index("bx"), lax.axis_index("by")
    core = (flip(bx, 1), by)
    x1 = (flip(bx, 2), by)
    x3 = (flip(flip(bx, 2), 4), by)
    z1 = (bx, flip(by, 4))
    z3 = (flip(bx, 8), flip(by, 4))
    y1 = (bx, flip(by, 1))
    y2 = (bx, flip(by, 2))

    def load(c):
        return pltpu.make_async_copy(x_ref.at[:, pl.ds(c, 1)], xv.at[:, pl.ds(c, 1)], load_sem.at[c])

    edges = pltpu.make_async_copy(edges_hbm, edges_ref, edges_sem)
    load(0).start()
    barrier = pltpu.get_barrier_semaphore()
    ring_x = (core, x1, x3, (flip(bx, 4), by))
    ring_x = ring_x + tuple((flip(device[0], 1), by) for device in ring_x[1:])
    ring_z = (z1, z3, (flip(bx, 8), by))
    ring_y = (y1, y2, (bx, flip(flip(by, 1), 2)))
    neighbours = ring_x + ring_z + ring_y
    for device in neighbours:
        pl.semaphore_signal(barrier, inc=1, device_id=device, device_id_type=MESH)

    edges.start()
    for c in range(1, windows):
        load(c).start()


    def copy(stream, c):
        src = {0: got.at[4, c], 1: got.at[2, c]}.get(stream, own.at[c])
        return pltpu.make_async_remote_copy(
            src_ref=src, dst_ref=got.at[stream, c], send_sem=send_sem.at[stream, c],
            recv_sem=recv_sem.at[stream, c], device_id=(z3, x3, x1, core, z1, y2)[stream], device_id_type=MESH)

    r = lax.broadcasted_iota(jnp.int32, (rows, rows), 0)
    k = lax.broadcasted_iota(jnp.int32, (rows, rows), 1)
    pick = jnp.where(k == nparts * (r % channels) + r // channels, 1.0, 0.0).astype(jnp.bfloat16)

    def prepare(c):
        block = xv[:, c].reshape(rows, nbins)
        own[c] = jnp.dot(pick, block, preferred_element_type=jnp.float32).astype(jnp.bfloat16)

    def send(c):
        if COMM:
            for stream in (2, 4, 5):
                copy(stream, c).start()

    def ready(c):
        prepare(c)
        if c == 0:
            pl.semaphore_wait(barrier, len(neighbours))
        if c < AHEAD:
            send(c)
        if COMM:
            copy(3, c).start()


    def measure():
        def squares(c, total):
            v = xv[:, c].reshape(rows, nbins).astype(jnp.float32)
            return total + jnp.sum((v * v).reshape(rows // 8, 8, nbins), axis=0)
        bins = lax.fori_loop(0, windows, squares, jnp.zeros((8, nbins), jnp.float32))
        bins = jnp.sum(bins, axis=0, keepdims=True)
        power[...] = jnp.broadcast_to(jnp.sum(mask * bins, axis=1, keepdims=True), power.shape)

    stages = (range(7), range(7, 10), range(10, 13))

    def exchange(i):
        stage = [i in s for s in stages].index(True)
        return pltpu.make_async_remote_copy(
            src_ref=parts.at[stage], dst_ref=parts.at[len(stages) + i], send_sem=psend_sem.at[i],
            recv_sem=precv_sem.at[i], device_id=neighbours[i], device_id_type=MESH)

    def begin(stage):
        parts[stages.index(stage)] = power[...]
        for i in stage:
            exchange(i).start()

    def end(stage):
        for i in stage:
            exchange(i).wait_recv()
            power[...] += parts[len(stages) + i]


    def build(c):
        for p in range(nparts):
            v = own[c, p * channels:(p + 1) * channels].astype(jnp.float32)
            wide = jnp.broadcast_to(v[:, None, :], (channels, bands, nbins)) * mask[None]
            left[c, :, p * nbins:(p + 1) * nbins] = wide.reshape(channels * bands, nbins).astype(jnp.bfloat16)

    def paired(r, c):
        cos, sin = got[r, c, :channels], got[r, c, channels:]
        return jnp.concatenate(
            [jnp.concatenate([cos, sin], axis=1), jnp.concatenate([-sin, cos], axis=1)], axis=0)

    def accumulate(r, c, norm=None, width=1, first=False):
        if not COMPUTE: return
        right = jnp.concatenate([paired(r, c + i) for i in range(width)], axis=1)
        wide = jnp.concatenate([left[c + i] for i in range(width)], axis=1)
        product = lax.dot_general(
            wide, right, (((1,), (1,)), ((), ())), preferred_element_type=jnp.float32)
        for p in range(2):
            value = product[:, p * channels:(p + 1) * channels].reshape(channels, bands, channels)
            if not first:
                value = acc_ref[:, r, p] + value
            if norm is not None:
                value = value * norm[None]
            acc_ref[:, r, p] = value

    def wait(stream, c):
        if COMM: copy(stream, c).wait_recv()

    def start(stream, c):
        if COMM: copy(stream, c).start()

    def advance(c):
        if COMM:
            @pl.when(c + AHEAD < windows)
            def _():
                send(c + AHEAD)
        wait(2, c)
        start(1, c)
        wait(4, c)
        start(0, c)

    def builds(first, count):
        if COMPUTE:
            @pl.loop(first, first + count)
            def _(c):
                build(c)

    def step(c, pair):
        for i in range(len(stages) - 1):
            @pl.when(c == AT[i])
            def _(i=i):
                end(stages[i])
                begin(stages[i + 1])
        advance(c)
        if pair:
            at = 2 * c - 2 * START
            wait(3, at)
            wait(3, at + 1)
        wait(5, c - 1)
        for r in (1, 0):
            wait(r, c - 2)
        for r in (2, 4, 5):
            accumulate(r, c - 1)
        for r in (1, 0):
            accumulate(r, c - 2)
        if pair:
            accumulate(3, at, width=2)

    load(0).wait()
    ready(0)
    edges.wait()
    mask = band_mask(edges_ref, bands, nbins)
    for c in range(1, windows):
        load(c).wait()
    measure()
    begin(stages[0])
    for c in range(1, EARLY):
        ready(c)
    advance(0)
    for c in range(EARLY, windows):
        ready(c)
    builds(0, 4)
    advance(1)
    wait(5, 0)
    for r in (2, 4, 5):
        accumulate(r, 0, first=True)
    acc_ref[:, 3] = jnp.zeros_like(acc_ref[:, 3])
    builds(4, 2)
    advance(2)
    wait(5, 1)
    for r in (1, 0):
        wait(r, 0)
    for r in (2, 4, 5):
        accumulate(r, 1)
    for r in (1, 0):
        accumulate(r, 0, first=True)
    builds(6, windows - 6)

    half = START + windows // 2
    @pl.loop(START, half)
    def _(c):
        step(c, True)

    @pl.loop(half, windows)
    def _(c):
        step(c, False)

    last = windows - 1
    end(stages[-1])
    norm = 1.0 / (power[...] / (count * windows) + EPS)
    wait(5, last)
    for r in (1, 0):
        wait(r, last - 1)
    for r in (2, 4, 5):
        accumulate(r, last, norm)
    for r in (1, 0):
        accumulate(r, last - 1)
    for p in range(2):
        acc_ref[:, 3, p] = acc_ref[:, 3, p] * norm[None]
    norm_ref[...] = norm
    wide_ref[...] = left[last]
    for r in (1, 0):
        wait(r, last)
        right_ref[r] = paired(r, last)

    if COMM:
        @pl.loop(0, windows)
        def _(c):
            for stream in range(ROUNDS):
                copy(stream, c).wait_send()
    for i in range(len(neighbours)):
        exchange(i).wait_send()


def finish(acc_ref, wide_ref, right_ref, norm_ref, out_ref, done, sems):
    channels, _, parts, bands, _ = acc_ref.shape
    count = done.shape[0]
    early = pltpu.make_async_copy(acc_ref.at[:, count:], out_ref.at[:, count:], sems.at[count])
    early.start()
    norm = norm_ref[...]
    late = []
    for r in range(count):
        product = lax.dot_general(
            wide_ref[...], right_ref[r], (((1,), (1,)), ((), ())), preferred_element_type=jnp.float32)
        for p in range(parts):
            value = product[:, p * channels:(p + 1) * channels].reshape(channels, bands, channels)
            done[r, :, p] = (acc_ref[:, r, p] + value) * norm[None]
        late.append(pltpu.make_async_copy(done.at[r], out_ref.at[:, r], sems.at[r]))
        late[-1].start()
    for copy in (early, *late):
        copy.wait()


def body(spectra, band_edges):
    channels, windows, parts, nbins = spectra.shape
    bands = band_edges.shape[0] - 1
    devices = lax.axis_size("bx") * lax.axis_size("by")
    rows = channels * parts
    dma = pltpu.SemaphoreType.DMA
    vmem = pltpu.VMEM
    results = pl.pallas_call(
        functools.partial(kernel, channels * devices),
        out_shape=(vmem((channels, ROUNDS, parts, bands, channels), jnp.float32),
                   vmem((channels * bands, parts * nbins), jnp.bfloat16),
                   vmem((2, rows, parts * nbins), jnp.bfloat16),
                   vmem((bands, 128), jnp.float32)),
        in_specs=[pl.BlockSpec(memory_space=pl.ANY), pl.BlockSpec(memory_space=pl.ANY)],
        out_specs=(pl.BlockSpec(memory_space=vmem),) * 4,
        scratch_shapes=[
            pltpu.SMEM(band_edges.shape, jnp.int32),
            vmem(spectra.shape, jnp.bfloat16),
            vmem((windows, rows, nbins), jnp.bfloat16),
            vmem((ROUNDS, windows, rows, nbins), jnp.bfloat16),
            vmem((windows, channels * bands, parts * nbins), jnp.bfloat16),
            vmem((bands, 128), jnp.float32),
            vmem((16, bands, 128), jnp.float32),
            dma(()), dma((windows,)), dma((ROUNDS, windows)), dma((ROUNDS, windows)), dma((13,)), dma((13,)),
        ],
        compiler_params=pltpu.CompilerParams(
            collective_id=0, has_side_effects=True, vmem_limit_bytes=52 * 2**20),
        name="exchange",
    )(band_edges, spectra)
    return pl.pallas_call(
        finish,
        out_shape=jax.ShapeDtypeStruct((channels, ROUNDS, parts, bands, channels), jnp.float32),
        in_specs=[pl.BlockSpec(memory_space=vmem)] * 4,
        out_specs=pl.BlockSpec(memory_space=pl.ANY),
        scratch_shapes=[vmem((2, channels, parts, bands, channels), jnp.float32), dma((3,))],
        compiler_params=pltpu.CompilerParams(vmem_limit_bytes=8 * 2**20),
        name="finish",
    )(*(pltpu.with_memory_space_constraint(value, vmem) for value in results))


def solution(mesh):
    return jax.shard_map(
        body,
        mesh=mesh,
        in_specs=(P(("bx", "by"), None, None, None), P()),
        out_specs=P(("bx", "by"), None, None, None, None),
        check_vma=False,
    )
```

```python
import functools
import jax
import jax.numpy as jnp
from jax import lax
from jax.experimental import pallas as pl
from jax.experimental.pallas import tpu as pltpu
from jax.sharding import PartitionSpec as P

ROUNDS = 6
EPS = 1e-06
MESH = pl.DeviceIdType.MESH
AHEAD = 2
EARLY = 4
AT = (3, 6)
START = 3
COMPUTE = True
COMM = True


def flip(index, bit):
    return index + bit - 2 * bit * ((index // bit) % 2)


def band_mask(edges_ref, bands, nbins):
    row = lax.broadcasted_iota(jnp.int32, (bands, nbins), 0)
    freq = lax.broadcasted_iota(jnp.int32, (bands, nbins), 1)
    low = jnp.zeros((bands, nbins), jnp.int32)
    high = jnp.zeros((bands, nbins), jnp.int32)
    for b in range(bands):
        low = jnp.where(row == b, edges_ref[b], low)
        high = jnp.where(row == b, edges_ref[b + 1], high)
    return jnp.where((freq >= low) & (freq < high), 1.0, 0.0).astype(jnp.float32)


def kernel(count, edges_hbm, x_ref, acc_ref, wide_ref, right_ref, norm_ref, edges_ref, xv, own, got, left, power, parts,
           edges_sem, load_sem, send_sem, recv_sem, psend_sem, precv_sem):
    channels, windows, nparts, nbins = xv.shape
    bands = power.shape[0]
    rows = nparts * channels
    bx, by = lax.axis_index("bx"), lax.axis_index("by")
    core = (flip(bx, 1), by)
    x1 = (flip(bx, 2), by)
    x3 = (flip(flip(bx, 2), 4), by)
    z1 = (bx, flip(by, 4))
    z3 = (flip(bx, 8), flip(by, 4))
    y1 = (bx, flip(by, 1))
    y2 = (bx, flip(by, 2))

    def load(c):
        return pltpu.make_async_copy(x_ref.at[:, pl.ds(c, 1)], xv.at[:, pl.ds(c, 1)], load_sem.at[c])

    edges = pltpu.make_async_copy(edges_hbm, edges_ref, edges_sem)
    load(0).start()
    barrier = pltpu.get_barrier_semaphore()
    ring_x = (core, x1, x3, (flip(bx, 4), by))
    ring_x = ring_x + tuple((flip(device[0], 1), by) for device in ring_x[1:])
    ring_z = (z1, z3, (flip(bx, 8), by))
    ring_y = (y1, y2, (bx, flip(flip(by, 1), 2)))
    neighbours = ring_x + ring_z + ring_y
    for device in neighbours:
        pl.semaphore_signal(barrier, inc=1, device_id=device, device_id_type=MESH)

    edges.start()
    for c in range(1, windows):
        load(c).start()


    def copy(stream, c):
        src = {0: got.at[4, c], 1: got.at[2, c]}.get(stream, own.at[c])
        return pltpu.make_async_remote_copy(
            src_ref=src, dst_ref=got.at[stream, c], send_sem=send_sem.at[stream, c],
            recv_sem=recv_sem.at[stream, c], device_id=(z3, x3, x1, core, z1, y2)[stream], device_id_type=MESH)

    r = lax.broadcasted_iota(jnp.int32, (rows, rows), 0)
    k = lax.broadcasted_iota(jnp.int32, (rows, rows), 1)
    pick = jnp.where(k == nparts * (r % channels) + r // channels, 1.0, 0.0).astype(jnp.bfloat16)

    def prepare(c):
        block = xv[:, c].reshape(rows, nbins)
        own[c] = jnp.dot(pick, block, preferred_element_type=jnp.float32).astype(jnp.bfloat16)

    def send(c):
        if COMM:
            for stream in (2, 4, 5):
                copy(stream, c).start()

    def ready(c):
        prepare(c)
        if c == 0:
            pl.semaphore_wait(barrier, len(neighbours))
        if c < AHEAD:
            send(c)
        if COMM:
            copy(3, c).start()


    def measure():
        def squares(c, total):
            v = xv[:, c].reshape(rows, nbins).astype(jnp.float32)
            return total + jnp.sum((v * v).reshape(rows // 8, 8, nbins), axis=0)
        bins = lax.fori_loop(0, windows, squares, jnp.zeros((8, nbins), jnp.float32))
        bins = jnp.sum(bins, axis=0, keepdims=True)
        power[...] = jnp.broadcast_to(jnp.sum(mask * bins, axis=1, keepdims=True), power.shape)

    stages = (range(7), range(7, 10), range(10, 13))

    def exchange(i):
        stage = [i in s for s in stages].index(True)
        return pltpu.make_async_remote_copy(
            src_ref=parts.at[stage], dst_ref=parts.at[len(stages) + i], send_sem=psend_sem.at[i],
            recv_sem=precv_sem.at[i], device_id=neighbours[i], device_id_type=MESH)

    def begin(stage):
        parts[stages.index(stage)] = power[...]
        for i in stage:
            exchange(i).start()

    def end(stage):
        for i in stage:
            exchange(i).wait_recv()
            power[...] += parts[len(stages) + i]


    def build(c):
        for p in range(nparts):
            v = own[c, p * channels:(p + 1) * channels].astype(jnp.float32)
            wide = jnp.broadcast_to(v[:, None, :], (channels, bands, nbins)) * mask[None]
            left[c, :, p * nbins:(p + 1) * nbins] = wide.reshape(channels * bands, nbins).astype(jnp.bfloat16)

    def paired(r, c):
        cos, sin = got[r, c, :channels], got[r, c, channels:]
        return jnp.concatenate(
            [jnp.concatenate([cos, sin], axis=1), jnp.concatenate([-sin, cos], axis=1)], axis=0)

    def accumulate(r, c, norm=None, width=1, first=False):
        if not COMPUTE: return
        right = jnp.concatenate([paired(r, c + i) for i in range(width)], axis=1)
        wide = jnp.concatenate([left[c + i] for i in range(width)], axis=1)
        product = lax.dot_general(
            wide, right, (((1,), (1,)), ((), ())), preferred_element_type=jnp.float32)
        for p in range(2):
            value = product[:, p * channels:(p + 1) * channels].reshape(channels, bands, channels)
            if not first:
                value = acc_ref[:, r, p] + value
            if norm is not None:
                value = value * norm[None]
            acc_ref[:, r, p] = value

    def wait(stream, c):
        if COMM: copy(stream, c).wait_recv()

    def start(stream, c):
        if COMM: copy(stream, c).start()

    def advance(c):
        wait(4, c)
        start(0, c)
        wait(2, c)
        start(1, c)
        if COMM:
            @pl.when(c + AHEAD < windows)
            def _():
                send(c + AHEAD)

    def builds(first, count):
        if COMPUTE:
            @pl.loop(first, first + count)
            def _(c):
                build(c)

    def step(c, pair):
        for i in range(len(stages) - 1):
            @pl.when(c == AT[i])
            def _(i=i):
                end(stages[i])
                begin(stages[i + 1])
        advance(c)
        if pair:
            at = 2 * c - 2 * START
            wait(3, at)
            wait(3, at + 1)
        wait(5, c - 1)
        for r in (1, 0):
            wait(r, c - 2)
        for r in (2, 4, 5):
            accumulate(r, c - 1)
        for r in (1, 0):
            accumulate(r, c - 2)
        if pair:
            accumulate(3, at, width=2)

    load(0).wait()
    ready(0)
    edges.wait()
    mask = band_mask(edges_ref, bands, nbins)
    for c in range(1, windows):
        load(c).wait()
    measure()
    begin(stages[0])
    for c in range(1, EARLY):
        ready(c)
    advance(0)
    for c in range(EARLY, windows):
        ready(c)
    builds(0, 4)
    advance(1)
    wait(5, 0)
    for r in (2, 4, 5):
        accumulate(r, 0, first=True)
    acc_ref[:, 3] = jnp.zeros_like(acc_ref[:, 3])
    builds(4, 2)
    advance(2)
    wait(5, 1)
    for r in (1, 0):
        wait(r, 0)
    for r in (2, 4, 5):
        accumulate(r, 1)
    for r in (1, 0):
        accumulate(r, 0, first=True)
    builds(6, windows - 6)

    half = START + windows // 2
    @pl.loop(START, half)
    def _(c):
        step(c, True)

    @pl.loop(half, windows)
    def _(c):
        step(c, False)

    last = windows - 1
    end(stages[-1])
    norm = 1.0 / (power[...] / (count * windows) + EPS)
    wait(5, last)
    for r in (1, 0):
        wait(r, last - 1)
    for r in (2, 4, 5):
        accumulate(r, last, norm)
    for r in (1, 0):
        accumulate(r, last - 1)
    for p in range(2):
        acc_ref[:, 3, p] = acc_ref[:, 3, p] * norm[None]
    norm_ref[...] = norm
    wide_ref[...] = left[last]
    for r in (1, 0):
        wait(r, last)
        right_ref[r] = paired(r, last)

    if COMM:
        @pl.loop(0, windows)
        def _(c):
            for stream in range(ROUNDS):
                copy(stream, c).wait_send()
    for i in range(len(neighbours)):
        exchange(i).wait_send()


def finish(acc_ref, wide_ref, right_ref, norm_ref, out_ref, done, sems):
    channels, _, parts, bands, _ = acc_ref.shape
    count = done.shape[0]
    early = pltpu.make_async_copy(acc_ref.at[:, count:], out_ref.at[:, count:], sems.at[count])
    early.start()
    norm = norm_ref[...]
    late = []
    for r in range(count):
        product = lax.dot_general(
            wide_ref[...], right_ref[r], (((1,), (1,)), ((), ())), preferred_element_type=jnp.float32)
        for p in range(parts):
            value = product[:, p * channels:(p + 1) * channels].reshape(channels, bands, channels)
            done[r, :, p] = (acc_ref[:, r, p] + value) * norm[None]
        late.append(pltpu.make_async_copy(done.at[r], out_ref.at[:, r], sems.at[r]))
        late[-1].start()
    for copy in (early, *late):
        copy.wait()


def body(spectra, band_edges):
    channels, windows, parts, nbins = spectra.shape
    bands = band_edges.shape[0] - 1
    devices = lax.axis_size("bx") * lax.axis_size("by")
    rows = channels * parts
    dma = pltpu.SemaphoreType.DMA
    vmem = pltpu.VMEM
    results = pl.pallas_call(
        functools.partial(kernel, channels * devices),
        out_shape=(vmem((channels, ROUNDS, parts, bands, channels), jnp.float32),
                   vmem((channels * bands, parts * nbins), jnp.bfloat16),
                   vmem((2, rows, parts * nbins), jnp.bfloat16),
                   vmem((bands, 128), jnp.float32)),
        in_specs=[pl.BlockSpec(memory_space=pl.ANY), pl.BlockSpec(memory_space=pl.ANY)],
        out_specs=(pl.BlockSpec(memory_space=vmem),) * 4,
        scratch_shapes=[
            pltpu.SMEM(band_edges.shape, jnp.int32),
            vmem(spectra.shape, jnp.bfloat16),
            vmem((windows, rows, nbins), jnp.bfloat16),
            vmem((ROUNDS, windows, rows, nbins), jnp.bfloat16),
            vmem((windows, channels * bands, parts * nbins), jnp.bfloat16),
            vmem((bands, 128), jnp.float32),
            vmem((16, bands, 128), jnp.float32),
            dma(()), dma((windows,)), dma((ROUNDS, windows)), dma((ROUNDS, windows)), dma((13,)), dma((13,)),
        ],
        compiler_params=pltpu.CompilerParams(
            collective_id=0, has_side_effects=True, vmem_limit_bytes=52 * 2**20),
        name="exchange",
    )(band_edges, spectra)
    return pl.pallas_call(
        finish,
        out_shape=jax.ShapeDtypeStruct((channels, ROUNDS, parts, bands, channels), jnp.float32),
        in_specs=[pl.BlockSpec(memory_space=vmem)] * 4,
        out_specs=pl.BlockSpec(memory_space=pl.ANY),
        scratch_shapes=[vmem((2, channels, parts, bands, channels), jnp.float32), dma((3,))],
        compiler_params=pltpu.CompilerParams(vmem_limit_bytes=8 * 2**20),
        name="finish",
    )(*(pltpu.with_memory_space_constraint(value, vmem) for value in results))


def solution(mesh):
    return jax.shard_map(
        body,
        mesh=mesh,
        in_specs=(P(("bx", "by"), None, None, None), P()),
        out_specs=P(("bx", "by"), None, None, None, None),
        check_vma=False,
    )
```

```python
import functools
import jax
import jax.numpy as jnp
from jax import lax
from jax.experimental import pallas as pl
from jax.experimental.pallas import tpu as pltpu
from jax.sharding import PartitionSpec as P

ROUNDS = 6
EPS = 1e-06
MESH = pl.DeviceIdType.MESH
AHEAD = 2
EARLY = 4
AT = (3, 6)
START = 3
COMPUTE = True
COMM = True


def flip(index, bit):
    return index + bit - 2 * bit * ((index // bit) % 2)


def band_mask(edges_ref, bands, nbins):
    row = lax.broadcasted_iota(jnp.int32, (bands, nbins), 0)
    freq = lax.broadcasted_iota(jnp.int32, (bands, nbins), 1)
    low = jnp.zeros((bands, nbins), jnp.int32)
    high = jnp.zeros((bands, nbins), jnp.int32)
    for b in range(bands):
        low = jnp.where(row == b, edges_ref[b], low)
        high = jnp.where(row == b, edges_ref[b + 1], high)
    return jnp.where((freq >= low) & (freq < high), 1.0, 0.0).astype(jnp.float32)


def kernel(count, edges_hbm, x_ref, acc_ref, wide_ref, right_ref, norm_ref, edges_ref, xv, own, got, left, power, parts,
           edges_sem, load_sem, send_sem, recv_sem, psend_sem, precv_sem):
    channels, windows, nparts, nbins = xv.shape
    bands = power.shape[0]
    rows = nparts * channels
    bx, by = lax.axis_index("bx"), lax.axis_index("by")
    core = (flip(bx, 1), by)
    x1 = (flip(bx, 2), by)
    x3 = (flip(flip(bx, 2), 4), by)
    z1 = (bx, flip(by, 4))
    z3 = (flip(bx, 8), flip(by, 4))
    y1 = (bx, flip(by, 1))
    y2 = (bx, flip(by, 2))

    def load(c):
        return pltpu.make_async_copy(x_ref.at[:, pl.ds(c, 1)], xv.at[:, pl.ds(c, 1)], load_sem.at[c])

    edges = pltpu.make_async_copy(edges_hbm, edges_ref, edges_sem)
    load(0).start()
    barrier = pltpu.get_barrier_semaphore()
    ring_x = (core, x1, x3, (flip(bx, 4), by))
    ring_x = ring_x + tuple((flip(device[0], 1), by) for device in ring_x[1:])
    ring_z = (z1, z3, (flip(bx, 8), by))
    ring_y = (y1, y2, (bx, flip(flip(by, 1), 2)))
    neighbours = ring_x + ring_z + ring_y
    for device in neighbours:
        pl.semaphore_signal(barrier, inc=1, device_id=device, device_id_type=MESH)

    edges.start()
    for c in range(1, windows):
        load(c).start()


    def copy(stream, c):
        src = {0: got.at[4, c], 1: got.at[2, c]}.get(stream, own.at[c])
        return pltpu.make_async_remote_copy(
            src_ref=src, dst_ref=got.at[stream, c], send_sem=send_sem.at[stream, c],
            recv_sem=recv_sem.at[stream, c], device_id=(z3, x3, x1, core, z1, y2)[stream], device_id_type=MESH)

    r = lax.broadcasted_iota(jnp.int32, (rows, rows), 0)
    k = lax.broadcasted_iota(jnp.int32, (rows, rows), 1)
    pick = jnp.where(k == nparts * (r % channels) + r // channels, 1.0, 0.0).astype(jnp.bfloat16)

    def prepare(c):
        block = xv[:, c].reshape(rows, nbins)
        own[c] = jnp.dot(pick, block, preferred_element_type=jnp.float32).astype(jnp.bfloat16)

    def send(c):
        if COMM:
            for stream in (2, 4, 5):
                copy(stream, c).start()

    def ready(c):
        prepare(c)
        if c == 0:
            pl.semaphore_wait(barrier, len(neighbours))
        if c < AHEAD:
            send(c)
        if COMM:
            copy(3, c).start()


    def measure():
        def squares(c, total):
            v = xv[:, c].reshape(rows, nbins).astype(jnp.float32)
            return total + jnp.sum((v * v).reshape(rows // 8, 8, nbins), axis=0)
        bins = lax.fori_loop(0, windows, squares, jnp.zeros((8, nbins), jnp.float32))
        bins = jnp.sum(bins, axis=0, keepdims=True)
        power[...] = jnp.broadcast_to(jnp.sum(mask * bins, axis=1, keepdims=True), power.shape)

    stages = (range(7), range(7, 10), range(10, 13))

    def exchange(i):
        stage = [i in s for s in stages].index(True)
        return pltpu.make_async_remote_copy(
            src_ref=parts.at[stage], dst_ref=parts.at[len(stages) + i], send_sem=psend_sem.at[i],
            recv_sem=precv_sem.at[i], device_id=neighbours[i], device_id_type=MESH)

    def begin(stage):
        parts[stages.index(stage)] = power[...]
        for i in stage:
            exchange(i).start()

    def end(stage):
        for i in stage:
            exchange(i).wait_recv()
            power[...] += parts[len(stages) + i]


    def build(c):
        for p in range(nparts):
            v = own[c, p * channels:(p + 1) * channels].astype(jnp.float32)
            wide = jnp.broadcast_to(v[:, None, :], (channels, bands, nbins)) * mask[None]
            left[c, :, p * nbins:(p + 1) * nbins] = wide.reshape(channels * bands, nbins).astype(jnp.bfloat16)

    def paired(r, c):
        cos, sin = got[r, c, :channels], got[r, c, channels:]
        return jnp.concatenate(
            [jnp.concatenate([cos, sin], axis=1), jnp.concatenate([-sin, cos], axis=1)], axis=0)

    def accumulate(r, c, norm=None, width=1, first=False):
        if not COMPUTE: return
        right = jnp.concatenate([paired(r, c + i) for i in range(width)], axis=1)
        wide = jnp.concatenate([left[c + i] for i in range(width)], axis=1)
        product = lax.dot_general(
            wide, right, (((1,), (1,)), ((), ())), preferred_element_type=jnp.float32)
        for p in range(2):
            value = product[:, p * channels:(p + 1) * channels].reshape(channels, bands, channels)
            if not first:
                value = acc_ref[:, r, p] + value
            if norm is not None:
                value = value * norm[None]
            acc_ref[:, r, p] = value

    def wait(stream, c):
        if COMM: copy(stream, c).wait_recv()

    def start(stream, c):
        if COMM: copy(stream, c).start()

    def advance(c):
        wait(4, c)
        start(0, c)
        wait(2, c)
        start(1, c)
        if COMM:
            @pl.when(c + AHEAD < windows)
            def _():
                send(c + AHEAD)

    def builds(first, count):
        if COMPUTE:
            @pl.loop(first, first + count)
            def _(c):
                build(c)

    def step(c, pair):
        for i in range(len(stages) - 1):
            @pl.when(c == AT[i])
            def _(i=i):
                end(stages[i])
                begin(stages[i + 1])
        advance(c)
        if pair:
            at = 2 * c - 2 * START
            wait(3, at)
            wait(3, at + 1)
        wait(5, c - 1)
        for r in (1, 0):
            wait(r, c - 2)
        for r in (2, 4, 5):
            accumulate(r, c - 1)
        for r in (1, 0):
            accumulate(r, c - 2)
        if pair:
            accumulate(3, at, width=2)

    load(0).wait()
    ready(0)
    edges.wait()
    mask = band_mask(edges_ref, bands, nbins)
    load(1).wait()
    ready(1)
    for c in range(2, windows):
        load(c).wait()
    measure()
    begin(stages[0])
    for c in range(2, EARLY):
        ready(c)
    advance(0)
    for c in range(EARLY, windows):
        ready(c)
    builds(0, 4)
    advance(1)
    wait(5, 0)
    for r in (2, 4, 5):
        accumulate(r, 0, first=True)
    acc_ref[:, 3] = jnp.zeros_like(acc_ref[:, 3])
    builds(4, 2)
    advance(2)
    wait(5, 1)
    for r in (1, 0):
        wait(r, 0)
    for r in (2, 4, 5):
        accumulate(r, 1)
    for r in (1, 0):
        accumulate(r, 0, first=True)
    builds(6, windows - 6)

    half = START + windows // 2
    @pl.loop(START, half)
    def _(c):
        step(c, True)

    @pl.loop(half, windows)
    def _(c):
        step(c, False)

    last = windows - 1
    end(stages[-1])
    norm = 1.0 / (power[...] / (count * windows) + EPS)
    wait(5, last)
    for r in (1, 0):
        wait(r, last - 1)
    for r in (2, 4, 5):
        accumulate(r, last, norm)
    for r in (1, 0):
        accumulate(r, last - 1)
    for p in range(2):
        acc_ref[:, 3, p] = acc_ref[:, 3, p] * norm[None]
    norm_ref[...] = norm
    wide_ref[...] = left[last]
    for r in (1, 0):
        wait(r, last)
        right_ref[r] = paired(r, last)

    if COMM:
        @pl.loop(0, windows)
        def _(c):
            for stream in range(ROUNDS):
                copy(stream, c).wait_send()
    for i in range(len(neighbours)):
        exchange(i).wait_send()


def finish(acc_ref, wide_ref, right_ref, norm_ref, out_ref, done, sems):
    channels, _, parts, bands, _ = acc_ref.shape
    count = done.shape[0]
    early = pltpu.make_async_copy(acc_ref.at[:, count:], out_ref.at[:, count:], sems.at[count])
    early.start()
    norm = norm_ref[...]
    late = []
    for r in range(count):
        product = lax.dot_general(
            wide_ref[...], right_ref[r], (((1,), (1,)), ((), ())), preferred_element_type=jnp.float32)
        for p in range(parts):
            value = product[:, p * channels:(p + 1) * channels].reshape(channels, bands, channels)
            done[r, :, p] = (acc_ref[:, r, p] + value) * norm[None]
        late.append(pltpu.make_async_copy(done.at[r], out_ref.at[:, r], sems.at[r]))
        late[-1].start()
    for copy in (early, *late):
        copy.wait()


def body(spectra, band_edges):
    channels, windows, parts, nbins = spectra.shape
    bands = band_edges.shape[0] - 1
    devices = lax.axis_size("bx") * lax.axis_size("by")
    rows = channels * parts
    dma = pltpu.SemaphoreType.DMA
    vmem = pltpu.VMEM
    results = pl.pallas_call(
        functools.partial(kernel, channels * devices),
        out_shape=(vmem((channels, ROUNDS, parts, bands, channels), jnp.float32),
                   vmem((channels * bands, parts * nbins), jnp.bfloat16),
                   vmem((2, rows, parts * nbins), jnp.bfloat16),
                   vmem((bands, 128), jnp.float32)),
        in_specs=[pl.BlockSpec(memory_space=pl.ANY), pl.BlockSpec(memory_space=pl.ANY)],
        out_specs=(pl.BlockSpec(memory_space=vmem),) * 4,
        scratch_shapes=[
            pltpu.SMEM(band_edges.shape, jnp.int32),
            vmem(spectra.shape, jnp.bfloat16),
            vmem((windows, rows, nbins), jnp.bfloat16),
            vmem((ROUNDS, windows, rows, nbins), jnp.bfloat16),
            vmem((windows, channels * bands, parts * nbins), jnp.bfloat16),
            vmem((bands, 128), jnp.float32),
            vmem((16, bands, 128), jnp.float32),
            dma(()), dma((windows,)), dma((ROUNDS, windows)), dma((ROUNDS, windows)), dma((13,)), dma((13,)),
        ],
        compiler_params=pltpu.CompilerParams(
            collective_id=0, has_side_effects=True, vmem_limit_bytes=52 * 2**20),
        name="exchange",
    )(band_edges, spectra)
    return pl.pallas_call(
        finish,
        out_shape=jax.ShapeDtypeStruct((channels, ROUNDS, parts, bands, channels), jnp.float32),
        in_specs=[pl.BlockSpec(memory_space=vmem)] * 4,
        out_specs=pl.BlockSpec(memory_space=pl.ANY),
        scratch_shapes=[vmem((2, channels, parts, bands, channels), jnp.float32), dma((3,))],
        compiler_params=pltpu.CompilerParams(vmem_limit_bytes=8 * 2**20),
        name="finish",
    )(*(pltpu.with_memory_space_constraint(value, vmem) for value in results))


def solution(mesh):
    return jax.shard_map(
        body,
        mesh=mesh,
        in_specs=(P(("bx", "by"), None, None, None), P()),
        out_specs=P(("bx", "by"), None, None, None, None),
        check_vma=False,
    )
```

```python
import functools
import jax
import jax.numpy as jnp
from jax import lax
from jax.experimental import pallas as pl
from jax.experimental.pallas import tpu as pltpu
from jax.sharding import PartitionSpec as P

ROUNDS = 6
EPS = 1e-06
MESH = pl.DeviceIdType.MESH
AHEAD = 3
EARLY = 5
AT = (3, 6)
START = 3
COMPUTE = True
COMM = True


def flip(index, bit):
    return index + bit - 2 * bit * ((index // bit) % 2)


def band_mask(edges_ref, bands, nbins):
    row = lax.broadcasted_iota(jnp.int32, (bands, nbins), 0)
    freq = lax.broadcasted_iota(jnp.int32, (bands, nbins), 1)
    low = jnp.zeros((bands, nbins), jnp.int32)
    high = jnp.zeros((bands, nbins), jnp.int32)
    for b in range(bands):
        low = jnp.where(row == b, edges_ref[b], low)
        high = jnp.where(row == b, edges_ref[b + 1], high)
    return jnp.where((freq >= low) & (freq < high), 1.0, 0.0).astype(jnp.float32)


def kernel(count, edges_hbm, x_ref, acc_ref, wide_ref, right_ref, norm_ref, edges_ref, xv, own, got, left, power, parts,
           edges_sem, load_sem, send_sem, recv_sem, psend_sem, precv_sem):
    channels, windows, nparts, nbins = xv.shape
    bands = power.shape[0]
    rows = nparts * channels
    bx, by = lax.axis_index("bx"), lax.axis_index("by")
    core = (flip(bx, 1), by)
    x1 = (flip(bx, 2), by)
    x3 = (flip(flip(bx, 2), 4), by)
    z1 = (bx, flip(by, 4))
    z3 = (flip(bx, 8), flip(by, 4))
    y1 = (bx, flip(by, 1))
    y2 = (bx, flip(by, 2))

    def load(c):
        return pltpu.make_async_copy(x_ref.at[:, pl.ds(c, 1)], xv.at[:, pl.ds(c, 1)], load_sem.at[c])

    edges = pltpu.make_async_copy(edges_hbm, edges_ref, edges_sem)
    load(0).start()
    barrier = pltpu.get_barrier_semaphore()
    ring_x = (core, x1, x3, (flip(bx, 4), by))
    ring_x = ring_x + tuple((flip(device[0], 1), by) for device in ring_x[1:])
    ring_z = (z1, z3, (flip(bx, 8), by))
    ring_y = (y1, y2, (bx, flip(flip(by, 1), 2)))
    neighbours = ring_x + ring_z + ring_y
    for device in neighbours:
        pl.semaphore_signal(barrier, inc=1, device_id=device, device_id_type=MESH)

    edges.start()
    for c in range(1, windows):
        load(c).start()


    def copy(stream, c):
        src = {0: got.at[4, c], 1: got.at[2, c]}.get(stream, own.at[c])
        return pltpu.make_async_remote_copy(
            src_ref=src, dst_ref=got.at[stream, c], send_sem=send_sem.at[stream, c],
            recv_sem=recv_sem.at[stream, c], device_id=(z3, x3, x1, core, z1, y2)[stream], device_id_type=MESH)

    r = lax.broadcasted_iota(jnp.int32, (rows, rows), 0)
    k = lax.broadcasted_iota(jnp.int32, (rows, rows), 1)
    pick = jnp.where(k == nparts * (r % channels) + r // channels, 1.0, 0.0).astype(jnp.bfloat16)

    def prepare(c):
        block = xv[:, c].reshape(rows, nbins)
        own[c] = jnp.dot(pick, block, preferred_element_type=jnp.float32).astype(jnp.bfloat16)

    def send(c):
        if COMM:
            for stream in (2, 4, 5):
                copy(stream, c).start()

    def ready(c):
        prepare(c)
        if c == 0:
            pl.semaphore_wait(barrier, len(neighbours))
        if c < AHEAD:
            send(c)
        if COMM:
            copy(3, c).start()


    def measure():
        def squares(c, total):
            v = xv[:, c].reshape(rows, nbins).astype(jnp.float32)
            return total + jnp.sum((v * v).reshape(rows // 8, 8, nbins), axis=0)
        bins = lax.fori_loop(0, windows, squares, jnp.zeros((8, nbins), jnp.float32))
        bins = jnp.sum(bins, axis=0, keepdims=True)
        power[...] = jnp.broadcast_to(jnp.sum(mask * bins, axis=1, keepdims=True), power.shape)

    stages = (range(7), range(7, 10), range(10, 13))

    def exchange(i):
        stage = [i in s for s in stages].index(True)
        return pltpu.make_async_remote_copy(
            src_ref=parts.at[stage], dst_ref=parts.at[len(stages) + i], send_sem=psend_sem.at[i],
            recv_sem=precv_sem.at[i], device_id=neighbours[i], device_id_type=MESH)

    def begin(stage):
        parts[stages.index(stage)] = power[...]
        for i in stage:
            exchange(i).start()

    def end(stage):
        for i in stage:
            exchange(i).wait_recv()
            power[...] += parts[len(stages) + i]


    def build(c):
        for p in range(nparts):
            v = own[c, p * channels:(p + 1) * channels].astype(jnp.float32)
            wide = jnp.broadcast_to(v[:, None, :], (channels, bands, nbins)) * mask[None]
            left[c, :, p * nbins:(p + 1) * nbins] = wide.reshape(channels * bands, nbins).astype(jnp.bfloat16)

    def paired(r, c):
        cos, sin = got[r, c, :channels], got[r, c, channels:]
        return jnp.concatenate(
            [jnp.concatenate([cos, sin], axis=1), jnp.concatenate([-sin, cos], axis=1)], axis=0)

    def accumulate(r, c, norm=None, width=1, first=False):
        if not COMPUTE: return
        right = jnp.concatenate([paired(r, c + i) for i in range(width)], axis=1)
        wide = jnp.concatenate([left[c + i] for i in range(width)], axis=1)
        product = lax.dot_general(
            wide, right, (((1,), (1,)), ((), ())), preferred_element_type=jnp.float32)
        for p in range(2):
            value = product[:, p * channels:(p + 1) * channels].reshape(channels, bands, channels)
            if not first:
                value = acc_ref[:, r, p] + value
            if norm is not None:
                value = value * norm[None]
            acc_ref[:, r, p] = value

    def wait(stream, c):
        if COMM: copy(stream, c).wait_recv()

    def start(stream, c):
        if COMM: copy(stream, c).start()

    def advance(c):
        wait(4, c)
        start(0, c)
        wait(2, c)
        start(1, c)
        if COMM:
            @pl.when(c + AHEAD < windows)
            def _():
                send(c + AHEAD)

    def builds(first, count):
        if COMPUTE:
            @pl.loop(first, first + count)
            def _(c):
                build(c)

    def step(c, pair):
        for i in range(len(stages) - 1):
            @pl.when(c == AT[i])
            def _(i=i):
                end(stages[i])
                begin(stages[i + 1])
        advance(c)
        if pair:
            at = 2 * c - 2 * START
            wait(3, at)
            wait(3, at + 1)
        wait(5, c - 1)
        for r in (1, 0):
            wait(r, c - 2)
        for r in (2, 4, 5):
            accumulate(r, c - 1)
        for r in (1, 0):
            accumulate(r, c - 2)
        if pair:
            accumulate(3, at, width=2)

    load(0).wait()
    ready(0)
    edges.wait()
    mask = band_mask(edges_ref, bands, nbins)
    load(1).wait()
    ready(1)
    for c in range(2, windows):
        load(c).wait()
    measure()
    begin(stages[0])
    for c in range(2, EARLY):
        ready(c)
    advance(0)
    for c in range(EARLY, windows):
        ready(c)
    builds(0, 4)
    advance(1)
    wait(5, 0)
    for r in (2, 4, 5):
        accumulate(r, 0, first=True)
    acc_ref[:, 3] = jnp.zeros_like(acc_ref[:, 3])
    builds(4, 2)
    advance(2)
    wait(5, 1)
    for r in (1, 0):
        wait(r, 0)
    for r in (2, 4, 5):
        accumulate(r, 1)
    for r in (1, 0):
        accumulate(r, 0, first=True)
    builds(6, windows - 6)

    half = START + windows // 2
    @pl.loop(START, half)
    def _(c):
        step(c, True)

    @pl.loop(half, windows)
    def _(c):
        step(c, False)

    last = windows - 1
    end(stages[-1])
    norm = 1.0 / (power[...] / (count * windows) + EPS)
    wait(5, last)
    for r in (1, 0):
        wait(r, last - 1)
    for r in (2, 4, 5):
        accumulate(r, last, norm)
    for r in (1, 0):
        accumulate(r, last - 1)
    for p in range(2):
        acc_ref[:, 3, p] = acc_ref[:, 3, p] * norm[None]
    norm_ref[...] = norm
    wide_ref[...] = left[last]
    for r in (1, 0):
        wait(r, last)
        right_ref[r] = paired(r, last)

    if COMM:
        @pl.loop(0, windows)
        def _(c):
            for stream in range(ROUNDS):
                copy(stream, c).wait_send()
    for i in range(len(neighbours)):
        exchange(i).wait_send()


def finish(acc_ref, wide_ref, right_ref, norm_ref, out_ref, done, sems):
    channels, _, parts, bands, _ = acc_ref.shape
    count = done.shape[0]
    early = pltpu.make_async_copy(acc_ref.at[:, count:], out_ref.at[:, count:], sems.at[count])
    early.start()
    norm = norm_ref[...]
    late = []
    for r in range(count):
        product = lax.dot_general(
            wide_ref[...], right_ref[r], (((1,), (1,)), ((), ())), preferred_element_type=jnp.float32)
        for p in range(parts):
            value = product[:, p * channels:(p + 1) * channels].reshape(channels, bands, channels)
            done[r, :, p] = (acc_ref[:, r, p] + value) * norm[None]
        late.append(pltpu.make_async_copy(done.at[r], out_ref.at[:, r], sems.at[r]))
        late[-1].start()
    for copy in (early, *late):
        copy.wait()


def body(spectra, band_edges):
    channels, windows, parts, nbins = spectra.shape
    bands = band_edges.shape[0] - 1
    devices = lax.axis_size("bx") * lax.axis_size("by")
    rows = channels * parts
    dma = pltpu.SemaphoreType.DMA
    vmem = pltpu.VMEM
    results = pl.pallas_call(
        functools.partial(kernel, channels * devices),
        out_shape=(vmem((channels, ROUNDS, parts, bands, channels), jnp.float32),
                   vmem((channels * bands, parts * nbins), jnp.bfloat16),
                   vmem((2, rows, parts * nbins), jnp.bfloat16),
                   vmem((bands, 128), jnp.float32)),
        in_specs=[pl.BlockSpec(memory_space=pl.ANY), pl.BlockSpec(memory_space=pl.ANY)],
        out_specs=(pl.BlockSpec(memory_space=vmem),) * 4,
        scratch_shapes=[
            pltpu.SMEM(band_edges.shape, jnp.int32),
            vmem(spectra.shape, jnp.bfloat16),
            vmem((windows, rows, nbins), jnp.bfloat16),
            vmem((ROUNDS, windows, rows, nbins), jnp.bfloat16),
            vmem((windows, channels * bands, parts * nbins), jnp.bfloat16),
            vmem((bands, 128), jnp.float32),
            vmem((16, bands, 128), jnp.float32),
            dma(()), dma((windows,)), dma((ROUNDS, windows)), dma((ROUNDS, windows)), dma((13,)), dma((13,)),
        ],
        compiler_params=pltpu.CompilerParams(
            collective_id=0, has_side_effects=True, vmem_limit_bytes=52 * 2**20),
        name="exchange",
    )(band_edges, spectra)
    return pl.pallas_call(
        finish,
        out_shape=jax.ShapeDtypeStruct((channels, ROUNDS, parts, bands, channels), jnp.float32),
        in_specs=[pl.BlockSpec(memory_space=vmem)] * 4,
        out_specs=pl.BlockSpec(memory_space=pl.ANY),
        scratch_shapes=[vmem((2, channels, parts, bands, channels), jnp.float32), dma((3,))],
        compiler_params=pltpu.CompilerParams(vmem_limit_bytes=8 * 2**20),
        name="finish",
    )(*(pltpu.with_memory_space_constraint(value, vmem) for value in results))


def solution(mesh):
    return jax.shard_map(
        body,
        mesh=mesh,
        in_specs=(P(("bx", "by"), None, None, None), P()),
        out_specs=P(("bx", "by"), None, None, None, None),
        check_vma=False,
    )
```
